32 devices in a mesh: groups: 2 (over x), wide: 16 (over z, y, core).
Axes of the slice: x: 2, y: 2, z: 4, core: 2. Of those that a mesh axis runs over, the one named last changes fastest.
Arguments:
- hidden_in: bfloat16 [32, 16384], P(('groups', 'wide')), parts along dimension 0, may hold values from -6 to 6
- norm_gain: float32 [16384], replicated, may hold values from 0.5 to 2
- query_weight: bfloat16 [16384, 16384], P(None, 'wide'), may hold values from -0.046875 to 0.046875
- kv_weight: bfloat16 [16384, 2048], P(None, 'wide'), may hold values from -0.046875 to 0.046875
- out_weight: bfloat16 [16384, 16384], P('wide'), may hold values from -0.75 to 0.75
- cache_keys: bfloat16 [32, 512, 1024], P(('groups', 'wide')), parts along dimension 0, may hold values from -64 to 64
- cache_values: bfloat16 [32, 512, 1024], P(('groups', 'wide')), parts along dimension 0, may hold values from -6 to 6
- lengths: int32 [32], P(('groups', 'wide')), parts along dimension 0, may hold values from 1 to 512, 5120 in all
- positions: int32 [32], P(('groups', 'wide')), parts along dimension 0, may hold values from 512 to 8191
Outputs:
- hidden_out: bfloat16 [32, 16384], P(('groups', 'wide')), parts along dimension 0
The draws below stay inside these ranges and needn't reach their ends.
There are 2 independent parts, one for each index of `groups`. The reference program is written for one: setup_inputs(seed, part) draws one part's arguments, and reference() takes and returns one part's arrays. A program takes and returns all parts, laid end to end along the dimension named above; an argument that names none is the same for every part. Nothing has to cross between parts.
Inputs may be any that keep to these rules, and one draw needn't show every extreme that they name: `lengths`: some request has all 512 slots filled.
All inputs are finite; a program needn't handle non-finite values. No bound on the sum of `lengths` on one device may be relied on, other than what follows from the above.
Results may differ from the reference program's by a relative error of at most 0.012.
The reference program's roundings to bfloat16 on the way count: a program that leaves them out, or rounds other values in their place, can miss the bound.
Values may be sent and summed in bfloat16 or wider, within the bound.
A program may use at most 192 MiB of HBM per device.

```python
import math
import jax
import jax.numpy as jnp
import numpy as np
from jax import lax

D = 16384
HQ = 128
KVH = 8
HD = 128
CACHE = 512
ROWS = 16
GROUP = 16


def draw_cache_keys(key, part):
    key = jax.random.fold_in(key, 11)
    base_key = jax.random.fold_in(key, 0)
    base = jnp.clip(jax.random.normal(base_key, (ROWS, CACHE, KVH * HD), jnp.float32), -6.0, 6.0)
    return base.astype(jnp.bfloat16)


def plant(drawn, own_key, least, high):
    dims = drawn.shape
    spot = [jax.random.randint(jax.random.fold_in(own_key, axis), (), 0, dims[axis]) for axis in range(len(dims))]
    drawn = drawn.at[tuple(spot)].set(least)
    longest = dims.index(max(dims))
    spot[longest] = (spot[longest] + 1) % dims[longest]
    return drawn.at[tuple(spot)].set(high)


def levels(own_key, shape, shards, low, largest):
    def one(dim, parts):
        draws = jax.random.uniform(jax.random.fold_in(jax.random.fold_in(own_key, 6), dim), (parts,), jnp.float32, low / len(shards), largest / len(shards))
        return jnp.repeat(jnp.exp(draws), shape[dim] // parts).reshape((-1,) + (1,) * (len(shape) - dim - 1))

    factor_of = one(*shards[0])
    for cut in shards[1:]:
        factor_of = factor_of * one(*cut)
    return factor_of


def profile(number_of, total, reach, skew):
    loads = [(1 << 20) // math.isqrt(rank ** skew) + 1 for rank in range(2, number_of + 1)]
    rest, given = total - reach - (number_of - 1), [1] * (number_of - 1)
    while rest > 0:
        free = [i for i in range(number_of - 1) if given[i] < reach]
        whole, left = sum([loads[i] for i in free]), rest
        for i in free:
            more = min(reach - given[i], max(1, left * loads[i] // whole), rest)
            given[i] = given[i] + more
            rest = rest - more
    return np.array([reach] + given)


def ragged(key, amount, total, limit, lean):
    if amount == 2:
        one = jax.random.randint(key, (), max(1, total - limit), min(limit, total - 1) + 1)
        return jnp.stack([one, total - one])
    sizes = jnp.asarray(profile(amount, total, limit, lean), jnp.int32)
    pairs = (amount - 1) // 2
    giver, sink = sizes[1:1 + 2 * pairs:2], sizes[2:2 + 2 * pairs:2]
    margin = jnp.minimum(giver - 1, limit - sink)
    passed = jax.random.randint(jax.random.fold_in(key, 1), (pairs,), 0, 1 << 20) % (margin + 1)
    sizes = sizes.at[1:1 + 2 * pairs:2].set(giver - passed).at[2:2 + 2 * pairs:2].set(sink + passed)
    return sizes[jax.random.permutation(jax.random.fold_in(key, 2), amount)]


def centred(stream_key, shape, scale, bound, shards=(), held_as=jnp.bfloat16):
    values = scale * jax.random.normal(stream_key, shape, jnp.float32)
    if shards:
        values = values * levels(stream_key, shape, shards, -0.22, 0.18)
    return jnp.clip(values, -bound, bound).astype(held_as)


def setup_inputs(seed: int = 0, part: int = 0) -> dict:
    seeds = jax.random.split(jax.random.key(seed), 10)
    part_keys = jax.random.split(jax.random.fold_in(seeds[9], part), 10)
    return {
        "hidden_in": centred(part_keys[0], (ROWS, D), 1.0, 6.0, ((0, 16),)),
        "norm_gain": jnp.clip(jnp.exp(jax.random.uniform(seeds[1], (D,), jnp.float32, math.log(0.5), math.log(2.0))), 0.5, 2.0),
        "query_weight": centred(seeds[2], (D, HQ * HD), D ** -0.5, 0.046875, ((1, 16),)),
        "kv_weight": centred(seeds[3], (D, 2 * KVH * HD), D ** -0.5, 0.046875, ((1, 16),)),
        "out_weight": centred(seeds[4], (HQ * HD, D), (HQ * HD * 2 // CACHE) ** -0.5, 0.75, ((0, 16),)),
        "cache_keys": draw_cache_keys(jax.random.fold_in(jax.random.fold_in(seeds[9], part), 71), part),
        "cache_values": centred(part_keys[6], (ROWS, CACHE, KVH * HD), 1.0, 6.0, ((0, 16),)),
        "lengths": ragged(part_keys[7], ROWS, ROWS * CACHE * 5 // 8, CACHE, 2).astype(jnp.int32),
        "positions": plant(jax.random.randint(part_keys[8], (ROWS,), CACHE, 8192), jax.random.fold_in(part_keys[8], 1), CACHE, 8191).astype(jnp.int32),
    }


def rms_scale(inputs_wide, norm_gain):
    spread = lax.optimization_barrier(jnp.mean(inputs_wide * inputs_wide, axis=-1, keepdims=True))
    return inputs_wide * lax.rsqrt(spread + 1e-05) * norm_gain

def rotary(values, places, head_count, head_size):
    grouped = values.reshape(values.shape[0], head_count, head_size)
    halfway = head_size // 2
    indices = jnp.arange(halfway).astype(jnp.float32)
    inverse = jnp.exp(indices * (-2.0 * math.log(500000.0) / head_size))
    angles = places.astype(jnp.float32)[:, None] * inverse[None, :]
    cosine = jnp.cos(angles)[:, None, :]
    sine = jnp.sin(angles)[:, None, :]
    first = grouped[..., :halfway]
    second = grouped[..., halfway:]
    turned = jnp.concatenate([first * cosine - second * sine, second * cosine + first * sine], axis=-1)
    return turned.reshape(values.shape)

def attend_block(inputs):
    query_turned, new_keys, new_values, old_keys, old_values, filled = inputs
    block_rows, slots = (old_keys.shape[0], old_keys.shape[1])
    factor = 1.0 / math.sqrt(HD)
    queries = query_turned.astype(jnp.float32).reshape(block_rows, KVH, GROUP, HD)
    keys_old = old_keys.astype(jnp.float32).reshape(block_rows, slots, KVH, HD)
    values_old = old_values.astype(jnp.float32).reshape(block_rows, slots, KVH, HD)
    keys_new = new_keys.astype(jnp.float32).reshape(block_rows, KVH, HD)
    values_new = new_values.astype(jnp.float32).reshape(block_rows, KVH, HD)
    cached_scores = jnp.einsum('rkgd,rlkd->rkgl', queries, keys_old) * factor
    fresh_scores = jnp.einsum('rkgd,rkd->rkg', queries, keys_new) * factor
    visible = jnp.arange(slots).astype(jnp.int32)[None, :] < filled[:, None]
    cached_scores = jnp.where(visible[:, None, None, :], cached_scores, -1e+30)
    highest = jnp.maximum(lax.optimization_barrier(jnp.max(cached_scores, axis=-1)), fresh_scores)
    cached_exp = jnp.exp(cached_scores - highest[..., None])
    fresh_exp = jnp.exp(fresh_scores - highest)
    totals = lax.optimization_barrier(jnp.sum(cached_exp, axis=-1)) + fresh_exp
    cached_weights = (cached_exp / totals[..., None]).astype(jnp.bfloat16).astype(jnp.float32)
    fresh_weights = (fresh_exp / totals).astype(jnp.bfloat16).astype(jnp.float32)
    mixed_values = jnp.einsum('rkgl,rlkd->rkgd', cached_weights, values_old)
    mixed_values = mixed_values + fresh_weights[..., None] * values_new[:, :, None, :]
    return mixed_values.reshape(block_rows, HQ * HD).astype(jnp.bfloat16)

def reference(hidden_in, norm_gain, query_weight, kv_weight, out_weight, cache_keys, cache_values, lengths, positions):
    inputs_wide = hidden_in.astype(jnp.float32)
    normed = rms_scale(inputs_wide, norm_gain).astype(jnp.bfloat16)
    query = jnp.dot(normed, query_weight, preferred_element_type=jnp.float32).astype(jnp.bfloat16)
    fresh = jnp.dot(normed, kv_weight, preferred_element_type=jnp.float32).astype(jnp.bfloat16)
    key_width = KVH * HD
    query_turned = rotary(query.astype(jnp.float32), positions, HQ, HD).astype(jnp.bfloat16)
    new_keys = rotary(fresh[:, :key_width].astype(jnp.float32), positions, KVH, HD).astype(jnp.bfloat16)
    new_values = fresh[:, key_width:]
    block_rows = 16
    blocks = ROWS // block_rows

    def split_rows(array):
        return array.reshape((blocks, block_rows) + array.shape[1:])
    attended = lax.map(attend_block, (split_rows(query_turned), split_rows(new_keys), split_rows(new_values), split_rows(cache_keys), split_rows(cache_values), split_rows(lengths)))
    attended = attended.reshape(ROWS, HQ * HD)
    summed = jnp.dot(attended, out_weight, preferred_element_type=jnp.float32)
    return (inputs_wide + summed).astype(jnp.bfloat16)
```

```python
import math

import jax
import jax.numpy as jnp
from jax import lax
from jax.experimental import pallas as pl
from jax.experimental.pallas import tpu as pltpu
from jax.sharding import PartitionSpec as P

HQ = 128
KVH = 8
HD = 128
GROUP = 16


def rms_scale(inputs_wide, norm_gain):
    spread = jnp.mean(inputs_wide * inputs_wide, axis=-1, keepdims=True)
    return inputs_wide * lax.rsqrt(spread + 1e-05) * norm_gain


def rotary(values, places, head_count, head_size):
    grouped = values.reshape(values.shape[0], head_count, head_size)
    halfway = head_size // 2
    indices = jnp.arange(halfway).astype(jnp.float32)
    inverse = jnp.exp(indices * (-2.0 * math.log(500000.0) / head_size))
    angles = places.astype(jnp.float32)[:, None] * inverse[None, :]
    cosine = jnp.cos(angles)[:, None, :]
    sine = jnp.sin(angles)[:, None, :]
    first = grouped[..., :halfway]
    second = grouped[..., halfway:]
    turned = jnp.concatenate(
        [first * cosine - second * sine, second * cosine + first * sine], axis=-1
    )
    return turned.reshape(values.shape)


def attend(query_rows, kv_rows, cache_keys, cache_values, lengths, positions):
    local_rows, slots = (cache_keys.shape[0], cache_keys.shape[1])
    group_size = HQ // KVH
    key_width = KVH * HD
    factor = 1.0 / math.sqrt(HD)
    queries = rotary(query_rows.astype(jnp.float32), positions, HQ, HD).astype(jnp.bfloat16)
    queries = queries.reshape(local_rows, KVH, group_size, HD)
    new_keys = rotary(kv_rows[:, :key_width].astype(jnp.float32), positions, KVH, HD).astype(
        jnp.bfloat16
    )
    new_keys = new_keys.reshape(local_rows, KVH, HD)
    new_values = kv_rows[:, key_width:].reshape(local_rows, KVH, HD)
    old_keys = cache_keys.reshape(local_rows, slots, KVH, HD)
    old_values = cache_values.reshape(local_rows, slots, KVH, HD)
    cached_scores = (
        jnp.einsum("rkgd,rlkd->rkgl", queries, old_keys, preferred_element_type=jnp.float32)
        * factor
    )
    fresh_scores = (
        jnp.einsum("rkgd,rkd->rkg", queries, new_keys, preferred_element_type=jnp.float32) * factor
    )
    visible = jnp.arange(slots)[None, :] < lengths[:, None]
    cached_scores = jnp.where(visible[:, None, None, :], cached_scores, -1e30)
    highest = jnp.maximum(jnp.max(cached_scores, axis=-1), fresh_scores)
    cached_exp = jnp.exp(cached_scores - highest[..., None])
    fresh_exp = jnp.exp(fresh_scores - highest)
    totals = jnp.sum(cached_exp, axis=-1) + fresh_exp
    cached_weights = (cached_exp / totals[..., None]).astype(jnp.bfloat16)
    fresh_weights = (fresh_exp / totals).astype(jnp.bfloat16)
    mixed_values = jnp.einsum(
        "rkgl,rlkd->rkgd", cached_weights, old_values, preferred_element_type=jnp.float32
    )
    mixed_values = (
        mixed_values
        + fresh_weights.astype(jnp.float32)[..., None]
        * new_values.astype(jnp.float32)[:, :, None, :]
    )
    return mixed_values.reshape(local_rows, HQ * HD).astype(jnp.bfloat16)


def per_device(
    hidden_in,
    norm_gain,
    query_weight,
    kv_weight,
    out_weight,
    cache_keys,
    cache_values,
    lengths,
    positions,
):
    inputs_wide = hidden_in.astype(jnp.float32)
    normed = rms_scale(inputs_wide, norm_gain).astype(jnp.bfloat16)
    query_cols = query_weight.shape[1]
    piece = lax.all_gather(normed, "wide", axis=0, tiled=True)
    query_part = jnp.dot(piece, query_weight, preferred_element_type=jnp.float32)
    fresh_part = jnp.dot(piece, kv_weight, preferred_element_type=jnp.float32)
    projected = jnp.concatenate([query_part, fresh_part], axis=1).astype(jnp.bfloat16)
    query_rows, kv_rows = (
        lax.all_to_all(projected[:, :query_cols], "wide", split_axis=0, concat_axis=1, tiled=True),
        lax.all_to_all(projected[:, query_cols:], "wide", split_axis=0, concat_axis=1, tiled=True),
    )
    attended = attend(query_rows, kv_rows, cache_keys, cache_values, lengths, positions)
    by_heads = lax.all_to_all(attended, "wide", split_axis=1, concat_axis=0, tiled=True)
    summed = lax.psum_scatter(
        jnp.dot(by_heads, out_weight, preferred_element_type=jnp.float32),
        "wide",
        scatter_dimension=0,
        tiled=True,
    )
    return (inputs_wide + summed).astype(jnp.bfloat16)


LINE, PAIR, CORES = 4, 2, 2
WIDE = LINE * PAIR * CORES
TILE = 1024
SLOTS = 24
LANES = 128
STEPS = 8


def remote(source, target, sent, landed, peer):
    return pltpu.make_async_remote_copy(
        src_ref=source,
        dst_ref=target,
        send_sem=sent,
        recv_sem=landed,
        device_id={"wide": peer},
        device_id_type=pl.DeviceIdType.MESH,
    )


def turn(values, cosine, sine):
    return values * cosine + pltpu.roll(values, HD // 2, 1) * sine


def fused_kernel(
    lengths,
    positions,
    hidden,
    gain,
    wq,
    wkv,
    wo,
    keys,
    values,
    out,
    ring,
    kv_held,
    keys_held,
    values_held,
    rows_f32,
    gain_f32,
    normed,
    tokens,
    total,
    message,
    message_out,
    message_in,
    heads_out,
    heads_in,
    mixed,
    partial,
    from_core,
    keep,
    pair_out,
    pair_in,
    line_out,
    line_in,
    ring_sem,
    kv_sem,
    cache_sem,
    norm_line_sent,
    norm_pair_sent,
    norm_core_sent,
    norm_landed,
    query_sent,
    query_landed,
    heads_sent,
    heads_landed,
    core_sent,
    core_landed,
    pair_sent,
    pair_landed,
    line_sent,
    line_landed,
):
    me = lax.axis_index("wide")
    core = lax.rem(me, CORES)
    row = lax.rem(me // CORES, PAIR)
    line = me // (CORES * PAIR)

    def at(a_line, a_row, a_core):
        return (a_line * PAIR + a_row) * CORES + a_core

    def by_core(place):
        return (
            lax.rem(place, CORES) * (PAIR * LINE)
            + lax.rem(place // CORES, PAIR) * LINE
            + place // (CORES * PAIR)
        )

    other_core = at(line, row, 1 - core)
    other_row = at(line, 1 - row, core)

    def other_line(step):
        return at(lax.rem(line + step, LINE), row, core)

    def query_block(index):
        return pltpu.make_async_copy(
            wq.at[pl.ds(index * TILE, TILE), :], ring.at[index], ring_sem.at[index]
        )

    def out_block(index):
        slot = lax.rem(index + 16, SLOTS)
        return pltpu.make_async_copy(
            wo.at[:, pl.ds(pl.multiple_of(index * TILE, TILE), TILE)],
            ring.at[slot],
            ring_sem.at[slot],
        )

    barrier = pltpu.get_barrier_semaphore()
    for step in range(1, WIDE):
        pl.semaphore_signal(
            barrier,
            inc=1,
            device_id={"wide": lax.rem(me + step, WIDE)},
            device_id_type=pl.DeviceIdType.MESH,
        )

    kv_copy = pltpu.make_async_copy(wkv, kv_held, kv_sem)
    kv_copy.start()
    for index in range(16):
        query_block(index).start()
    keys_copy = pltpu.make_async_copy(keys.at[0], keys_held, cache_sem.at[0])
    values_copy = pltpu.make_async_copy(values.at[0], values_held, cache_sem.at[1])
    keys_copy.start()
    values_copy.start()
    for index in range(SLOTS - 16):
        out_block(index).start()

    for part in range(16):
        span = slice(part * TILE, (part + 1) * TILE)
        rows_f32[part : part + 1, :] = hidden[:, span].astype(jnp.float32)
        gain_f32[part : part + 1, :] = gain[:, span]
    token = rows_f32[...]
    spread = jnp.sum(token * token, keepdims=True) * (1.0 / (16 * TILE))
    normed[me] = (token * lax.rsqrt(spread + 1e-05) * gain_f32[...]).astype(jnp.bfloat16)
    pl.semaphore_wait(barrier, WIDE - 1)

    def gather_line(step):
        return remote(
            normed.at[me],
            normed.at[me],
            norm_line_sent.at[step - 1],
            norm_landed.at[me],
            other_line(step),
        )

    def gather_pair(step):
        place = other_line(step)
        return remote(
            normed.at[place],
            normed.at[place],
            norm_pair_sent.at[step],
            norm_landed.at[place],
            other_row,
        )

    def gather_core(step, a_row):
        place = at(lax.rem(line + step, LINE), a_row, core)
        return remote(
            normed.at[place],
            normed.at[place],
            norm_core_sent.at[step * PAIR + a_row],
            norm_landed.at[place],
            other_core,
        )

    def landed(place):
        remote(
            normed.at[place],
            normed.at[place],
            norm_pair_sent.at[0],
            norm_landed.at[place],
            other_row,
        ).wait_recv()

    def spread_rows(place):
        block = normed[place].astype(jnp.float32)
        for part in range(TILE // LANES):
            tokens[part, pl.ds(place, 16, stride=16), :] = block[:, part * LANES : (part + 1) * LANES]

    for step in (2, 1, 3):
        gather_line(step).start()
    gather_pair(0).start()
    gather_core(0, row).start()
    spread_rows(me)
    for step in (1, 3, 2):
        landed(other_line(step))
        gather_pair(step).start()
        gather_core(step, row).start()
        spread_rows(other_line(step))
    for step in (0, 1, 3, 2):
        place = at(lax.rem(line + step, LINE), 1 - row, core)
        landed(place)
        gather_core(step, 1 - row).start()
        spread_rows(place)
    for step in range(LINE):
        for a_row in range(PAIR):
            place = at(lax.rem(line + step, LINE), a_row, 1 - core)
            landed(place)
            spread_rows(place)

    total[...] = jnp.zeros_like(total)
    message[...] = jnp.zeros_like(message)
    kv_copy.wait()

    def project(index, carry):
        rows = pl.ds(pl.multiple_of(index * 16, 16), 16)
        tile = jnp.concatenate([tokens[part, rows, :] for part in range(TILE // LANES)], axis=1)
        tile = tile.astype(jnp.bfloat16)
        total[:, TILE:] += jnp.dot(
            tile,
            kv_held[pl.ds(pl.multiple_of(index * TILE, TILE), TILE), :],
            preferred_element_type=jnp.float32,
        )
        query_block(index).wait()
        total[:, :TILE] += jnp.dot(tile, ring[index], preferred_element_type=jnp.float32)

        @pl.when(index < 32 - SLOTS)
        def _():
            out_block(index + SLOTS - 16).start()

        return carry

    lax.fori_loop(0, 16, project, 0)
    for part in range(9):
        message[pl.ds(part, 16, stride=16), :] = total[:, part * LANES : (part + 1) * LANES]
    message_out[...] = message[...].astype(jnp.bfloat16).reshape(WIDE, 16, LANES)

    def query_copy(step):
        peer = lax.rem(me + step, WIDE)
        return remote(
            message_out.at[peer],
            message_in.at[me],
            query_sent.at[step],
            query_landed.at[me],
            peer,
        )

    for step in range(1, WIDE):
        query_copy(step).start()
    message_in[me] = message_out[me]

    index = lax.broadcasted_iota(jnp.int32, (1, HD), 1)
    lower = index < HD // 2
    exponent = jnp.where(lower, index, index - HD // 2).astype(jnp.float32)
    inverse = jnp.exp(exponent * (-2.0 * math.log(500000.0) / HD))
    angle = positions[0].astype(jnp.float32) * inverse
    cosine = jnp.cos(angle)
    sine = jnp.sin(angle)
    sine = jnp.where(lower, -sine, sine)
    visible = lax.broadcasted_iota(jnp.int32, (GROUP, keys_held.shape[0]), 1) < lengths[0]
    factor = 1.0 / math.sqrt(HD)
    keys_copy.wait()
    values_copy.wait()
    for step in range(1, WIDE):
        place = lax.rem(me + step, WIDE)
        remote(
            message_out.at[place],
            message_in.at[place],
            query_sent.at[step],
            query_landed.at[place],
            place,
        ).wait_recv()
    for head in range(KVH):
        span = slice(head * HD, (head + 1) * HD)
        one = message_in[2 * head].astype(jnp.float32)
        two = message_in[2 * head + 1].astype(jnp.float32)
        query = turn(jnp.concatenate([one[:8], two[:8]], axis=0), cosine, sine).astype(jnp.bfloat16)
        new_key = message_in[head].astype(jnp.float32)[8:]
        new_key = turn(new_key, cosine, sine)[:1].astype(jnp.bfloat16).astype(jnp.float32)
        new_value = message_in[KVH + head].astype(jnp.float32)[8:9]
        scores = factor * lax.dot_general(
            query,
            keys_held[:, span],
            (((1,), (1,)), ((), ())),
            preferred_element_type=jnp.float32,
        )
        scores = jnp.where(visible, scores, -1e30)
        fresh = factor * jnp.sum(query.astype(jnp.float32) * new_key, axis=1, keepdims=True)
        highest = jnp.maximum(jnp.max(scores, axis=1, keepdims=True), fresh)
        raised = jnp.exp(scores - highest)
        fresh = jnp.exp(fresh - highest)
        whole = jnp.sum(raised, axis=1, keepdims=True) + fresh
        weights = (raised / whole).astype(jnp.bfloat16)
        fresh = (fresh / whole).astype(jnp.bfloat16).astype(jnp.float32)
        attended = jnp.dot(weights, values_held[:, span], preferred_element_type=jnp.float32)
        attended = (attended + fresh * new_value).astype(jnp.bfloat16).astype(jnp.float32)
        heads_out[2 * head] = attended[:8]
        heads_out[2 * head + 1] = attended[8:]

    def heads_copy(step):
        peer = lax.rem(me + step, WIDE)
        return remote(
            heads_out.at[peer],
            heads_in.at[pl.ds(pl.multiple_of(by_core(me) * 8, 8), 8), :],
            heads_sent.at[step],
            heads_landed.at[me],
            peer,
        )

    for step in range(1, WIDE):
        heads_copy(step).start()
    heads_in[pl.ds(pl.multiple_of(by_core(me) * 8, 8), 8), :] = heads_out[me]
    for step in range(1, WIDE):
        place = lax.rem(me + step, WIDE)
        remote(
            heads_out.at[place],
            heads_in.at[pl.ds(pl.multiple_of(by_core(place) * 8, 8), 8), :],
            heads_sent.at[step],
            heads_landed.at[place],
            place,
        ).wait_recv()
    mixed[...] = jnp.concatenate(
        [heads_in[pl.ds(part, 16, stride=8), :] for part in range(8)], axis=1
    ).astype(jnp.bfloat16)

    half = 8 * 16
    quarter = 4 * 16

    def core_copy(chunk):
        away = pl.ds(pl.multiple_of((1 - core) * half, half), half)
        return remote(
            partial.at[chunk, away, :],
            from_core.at[chunk],
            core_sent.at[chunk],
            core_landed.at[chunk],
            other_core,
        )

    def pair_copy(chunk):
        return remote(
            pair_out.at[chunk],
            pair_in.at[chunk],
            pair_sent.at[chunk],
            pair_landed.at[chunk],
            other_row,
        )

    def line_copy(chunk, step):
        goal = lax.rem(line + step, LINE)
        return remote(
            line_out.at[chunk, goal],
            line_in.at[chunk, step - 1],
            line_sent.at[chunk, step - 1],
            line_landed.at[chunk, step - 1],
            other_line(step),
        )

    def multiply(chunk):
        for side in range(2):
            number = chunk * 2 + side
            out_block(number).wait()
            slot = lax.rem(number + 16, SLOTS)
            product = jnp.dot(mixed[...], ring[slot], preferred_element_type=jnp.float32)
            for part in range(TILE // LANES):
                partial[chunk, pl.ds(side * 8 + part, 16, stride=16), :] = product[
                    :, part * LANES : (part + 1) * LANES
                ]
        core_copy(chunk).start()

    def over_cores(chunk):
        core_copy(chunk).wait_recv()
        away, home = (1 - row) * quarter, row * quarter
        base = core * half
        pair_out[chunk] = (
            partial[chunk, pl.ds(pl.multiple_of(base + away, quarter), quarter), :]
            + from_core[chunk, pl.ds(pl.multiple_of(away, quarter), quarter), :]
        ).astype(jnp.bfloat16)
        pair_copy(chunk).start()
        keep[chunk] = (
            partial[chunk, pl.ds(pl.multiple_of(base + home, quarter), quarter), :]
            + from_core[chunk, pl.ds(pl.multiple_of(home, quarter), quarter), :]
        )

    def over_pair(chunk):
        pair_copy(chunk).wait_recv()
        added = keep[chunk] + pair_in[chunk].astype(jnp.float32)
        keep[chunk] = added
        line_out[chunk] = added.astype(jnp.bfloat16).reshape(LINE, 16, LANES)
        for step in (2, 1, 3):
            line_copy(chunk, step).start()

    def over_line(chunk):
        for step in range(1, LINE):
            line_copy(chunk, step).wait_recv()
        added = keep[chunk, pl.ds(pl.multiple_of(line * 16, 16), 16), :]
        for step in range(1, LINE):
            added = added + line_in[chunk, step - 1].astype(jnp.float32)
        out[pl.ds(pl.multiple_of(chunk * 16, 16), 16), :] = added

    def stage(time, carry):
        pl.when(time < STEPS)(lambda: multiply(time))
        pl.when((time >= 1) & (time < STEPS + 1))(lambda: over_cores(time - 1))
        pl.when((time >= 2) & (time < STEPS + 2))(lambda: over_pair(time - 2))
        pl.when(time >= 3)(lambda: over_line(time - 3))
        return carry

    lax.fori_loop(0, STEPS + 3, stage, 0)

    for step in range(1, LINE):
        gather_line(step).wait_send()
    for step in range(LINE):
        gather_pair(step).wait_send()
        for a_row in range(PAIR):
            gather_core(step, a_row).wait_send()
    for step in range(1, WIDE):
        query_copy(step).wait_send()
        heads_copy(step).wait_send()

    def drain(chunk, carry):
        core_copy(chunk).wait_send()
        pair_copy(chunk).wait_send()
        for step in range(1, LINE):
            line_copy(chunk, step).wait_send()
        return carry

    lax.fori_loop(0, STEPS, drain, 0)


def per_device_fused(
    hidden_in,
    norm_gain,
    query_weight,
    kv_weight,
    out_weight,
    cache_keys,
    cache_values,
    lengths,
    positions,
):
    slots = cache_keys.shape[1]
    f32, bf16 = jnp.float32, jnp.bfloat16
    vmem, dma = pltpu.VMEM, pltpu.SemaphoreType.DMA
    summed = pl.pallas_call(
        fused_kernel,
        out_shape=jax.ShapeDtypeStruct((LANES, LANES), f32),
        in_specs=[pl.BlockSpec(memory_space=pltpu.SMEM)] * 2
        + [pl.BlockSpec(memory_space=pltpu.VMEM)] * 2
        + [pl.BlockSpec(memory_space=pl.ANY)] * 5,
        out_specs=pl.BlockSpec(memory_space=pltpu.VMEM),
        scratch_shapes=[
            vmem((SLOTS, TILE, TILE), bf16),
            vmem((16 * TILE, LANES), bf16),
            vmem((slots, KVH * HD), bf16),
            vmem((slots, KVH * HD), bf16),
            vmem((16, TILE), f32),
            vmem((16, TILE), f32),
            vmem((WIDE, 16, TILE), bf16),
            vmem((TILE // LANES, 256, LANES), f32),
            vmem((16, TILE + LANES), f32),
            vmem((WIDE * 16, LANES), f32),
            vmem((WIDE, 16, LANES), bf16),
            vmem((WIDE, 16, LANES), bf16),
            vmem((WIDE, 8, LANES), f32),
            vmem((WIDE * 8, LANES), f32),
            vmem((16, TILE), bf16),
            vmem((STEPS, 256, LANES), f32),
            vmem((STEPS, 128, LANES), f32),
            vmem((STEPS, 64, LANES), f32),
            vmem((STEPS, 64, LANES), bf16),
            vmem((STEPS, 64, LANES), bf16),
            vmem((STEPS, LINE, 16, LANES), bf16),
            vmem((STEPS, LINE - 1, 16, LANES), bf16),
            dma((SLOTS,)),
            dma,
            dma((2,)),
            dma((LINE - 1,)),
            dma((LINE,)),
            dma((LINE * PAIR,)),
            dma((WIDE,)),
            dma((WIDE,)),
            dma((WIDE,)),
            dma((WIDE,)),
            dma((WIDE,)),
            dma((STEPS,)),
            dma((STEPS,)),
            dma((STEPS,)),
            dma((STEPS,)),
            dma((STEPS, LINE - 1)),
            dma((STEPS, LINE - 1)),
        ],
        compiler_params=pltpu.CompilerParams(
            collective_id=0, has_side_effects=True, vmem_limit_bytes=62 * 1024 * 1024
        ),
        name="decode_attention",
    )(
        lengths,
        positions,
        hidden_in,
        norm_gain.reshape(1, -1),
        query_weight,
        kv_weight,
        out_weight,
        cache_keys,
        cache_values,
    )
    return (hidden_in.astype(f32) + summed.reshape(1, -1)).astype(bf16)


def solution(mesh):
    body = per_device_fused if mesh.shape["wide"] == WIDE else per_device
    return jax.shard_map(
        body,
        mesh=mesh,
        in_specs=(
            P(("groups", "wide"), None),
            P(),
            P(None, "wide"),
            P(None, "wide"),
            P("wide", None),
            P(("groups", "wide"), None, None),
            P(("groups", "wide"), None, None),
            P(("groups", "wide")),
            P(("groups", "wide")),
        ),
        out_specs=P(("groups", "wide"), None),
        check_vma=False,
    )
```

```python
import math

import jax
import jax.numpy as jnp
from jax import lax
from jax.experimental import pallas as pl
from jax.experimental.pallas import tpu as pltpu
from jax.sharding import PartitionSpec as P

HQ = 128
KVH = 8
HD = 128
GROUP = 16


def rms_scale(inputs_wide, norm_gain):
    spread = jnp.mean(inputs_wide * inputs_wide, axis=-1, keepdims=True)
    return inputs_wide * lax.rsqrt(spread + 1e-05) * norm_gain


def rotary(values, places, head_count, head_size):
    grouped = values.reshape(values.shape[0], head_count, head_size)
    halfway = head_size // 2
    indices = jnp.arange(halfway).astype(jnp.float32)
    inverse = jnp.exp(indices * (-2.0 * math.log(500000.0) / head_size))
    angles = places.astype(jnp.float32)[:, None] * inverse[None, :]
    cosine = jnp.cos(angles)[:, None, :]
    sine = jnp.sin(angles)[:, None, :]
    first = grouped[..., :halfway]
    second = grouped[..., halfway:]
    turned = jnp.concatenate(
        [first * cosine - second * sine, second * cosine + first * sine], axis=-1
    )
    return turned.reshape(values.shape)


def attend(query_rows, kv_rows, cache_keys, cache_values, lengths, positions):
    local_rows, slots = (cache_keys.shape[0], cache_keys.shape[1])
    group_size = HQ // KVH
    key_width = KVH * HD
    factor = 1.0 / math.sqrt(HD)
    queries = rotary(query_rows.astype(jnp.float32), positions, HQ, HD).astype(jnp.bfloat16)
    queries = queries.reshape(local_rows, KVH, group_size, HD)
    new_keys = rotary(kv_rows[:, :key_width].astype(jnp.float32), positions, KVH, HD).astype(
        jnp.bfloat16
    )
    new_keys = new_keys.reshape(local_rows, KVH, HD)
    new_values = kv_rows[:, key_width:].reshape(local_rows, KVH, HD)
    old_keys = cache_keys.reshape(local_rows, slots, KVH, HD)
    old_values = cache_values.reshape(local_rows, slots, KVH, HD)
    cached_scores = (
        jnp.einsum("rkgd,rlkd->rkgl", queries, old_keys, preferred_element_type=jnp.float32)
        * factor
    )
    fresh_scores = (
        jnp.einsum("rkgd,rkd->rkg", queries, new_keys, preferred_element_type=jnp.float32) * factor
    )
    visible = jnp.arange(slots)[None, :] < lengths[:, None]
    cached_scores = jnp.where(visible[:, None, None, :], cached_scores, -1e30)
    highest = jnp.maximum(jnp.max(cached_scores, axis=-1), fresh_scores)
    cached_exp = jnp.exp(cached_scores - highest[..., None])
    fresh_exp = jnp.exp(fresh_scores - highest)
    totals = jnp.sum(cached_exp, axis=-1) + fresh_exp
    cached_weights = (cached_exp / totals[..., None]).astype(jnp.bfloat16)
    fresh_weights = (fresh_exp / totals).astype(jnp.bfloat16)
    mixed_values = jnp.einsum(
        "rkgl,rlkd->rkgd", cached_weights, old_values, preferred_element_type=jnp.float32
    )
    mixed_values = (
        mixed_values
        + fresh_weights.astype(jnp.float32)[..., None]
        * new_values.astype(jnp.float32)[:, :, None, :]
    )
    return mixed_values.reshape(local_rows, HQ * HD).astype(jnp.bfloat16)


def per_device(
    hidden_in,
    norm_gain,
    query_weight,
    kv_weight,
    out_weight,
    cache_keys,
    cache_values,
    lengths,
    positions,
):
    inputs_wide = hidden_in.astype(jnp.float32)
    normed = rms_scale(inputs_wide, norm_gain).astype(jnp.bfloat16)
    query_cols = query_weight.shape[1]
    piece = lax.all_gather(normed, "wide", axis=0, tiled=True)
    query_part = jnp.dot(piece, query_weight, preferred_element_type=jnp.float32)
    fresh_part = jnp.dot(piece, kv_weight, preferred_element_type=jnp.float32)
    projected = jnp.concatenate([query_part, fresh_part], axis=1).astype(jnp.bfloat16)
    query_rows, kv_rows = (
        lax.all_to_all(projected[:, :query_cols], "wide", split_axis=0, concat_axis=1, tiled=True),
        lax.all_to_all(projected[:, query_cols:], "wide", split_axis=0, concat_axis=1, tiled=True),
    )
    attended = attend(query_rows, kv_rows, cache_keys, cache_values, lengths, positions)
    by_heads = lax.all_to_all(attended, "wide", split_axis=1, concat_axis=0, tiled=True)
    summed = lax.psum_scatter(
        jnp.dot(by_heads, out_weight, preferred_element_type=jnp.float32),
        "wide",
        scatter_dimension=0,
        tiled=True,
    )
    return (inputs_wide + summed).astype(jnp.bfloat16)


LINE, PAIR, CORES = 4, 2, 2
WIDE = LINE * PAIR * CORES
TILE = 1024
SLOTS = 24
LANES = 128
STEPS = 8
LAGS = (2, 5, 8)


def remote(source, target, sent, landed, peer):
    return pltpu.make_async_remote_copy(
        src_ref=source,
        dst_ref=target,
        send_sem=sent,
        recv_sem=landed,
        device_id={"wide": peer},
        device_id_type=pl.DeviceIdType.MESH,
    )


def turn(values, cosine, sine):
    return values * cosine + pltpu.roll(values, HD // 2, 1) * sine


def fused_kernel(
    lengths,
    positions,
    hidden,
    gain,
    wq,
    wkv,
    wo,
    keys,
    values,
    out,
    ring,
    kv_held,
    keys_held,
    values_held,
    rows_f32,
    gain_f32,
    normed,
    tokens,
    total,
    message,
    message_out,
    message_in,
    scores,
    heads_out,
    heads_in,
    mixed,
    partial,
    from_core,
    keep,
    pair_out,
    pair_in,
    line_out,
    line_in,
    ring_sem,
    kv_sem,
    cache_sem,
    norm_line_sent,
    norm_pair_sent,
    norm_core_sent,
    norm_landed,
    query_sent,
    query_landed,
    heads_sent,
    heads_landed,
    core_sent,
    core_landed,
    pair_sent,
    pair_landed,
    line_sent,
    line_landed,
):
    me = lax.axis_index("wide")
    core = lax.rem(me, CORES)
    row = lax.rem(me // CORES, PAIR)
    line = me // (CORES * PAIR)

    def at(a_line, a_row, a_core):
        return (a_line * PAIR + a_row) * CORES + a_core

    def by_core(place):
        return (
            lax.rem(place, CORES) * (PAIR * LINE)
            + lax.rem(place // CORES, PAIR) * LINE
            + place // (CORES * PAIR)
        )

    other_core = at(line, row, 1 - core)
    other_row = at(line, 1 - row, core)

    def other_line(step):
        return at(lax.rem(line + step, LINE), row, core)

    def query_block(index):
        return pltpu.make_async_copy(
            wq.at[pl.ds(index * TILE, TILE), :], ring.at[index], ring_sem.at[index]
        )

    def out_block(index):
        slot = lax.rem(index + 16, SLOTS)
        return pltpu.make_async_copy(
            wo.at[:, pl.ds(pl.multiple_of(index * TILE, TILE), TILE)],
            ring.at[slot],
            ring_sem.at[slot],
        )

    barrier = pltpu.get_barrier_semaphore()
    for step in range(1, WIDE):
        pl.semaphore_signal(
            barrier,
            inc=1,
            device_id={"wide": lax.rem(me + step, WIDE)},
            device_id_type=pl.DeviceIdType.MESH,
        )

    kv_copy = pltpu.make_async_copy(wkv, kv_held, kv_sem)
    kv_copy.start()
    for index in range(16):
        query_block(index).start()
    keys_copy = pltpu.make_async_copy(keys.at[0], keys_held, cache_sem.at[0])
    values_copy = pltpu.make_async_copy(values.at[0], values_held, cache_sem.at[1])
    keys_copy.start()
    values_copy.start()
    for index in range(SLOTS - 16):
        out_block(index).start()

    for part in range(16):
        span = slice(part * TILE, (part + 1) * TILE)
        rows_f32[part : part + 1, :] = hidden[:, span].astype(jnp.float32)
        gain_f32[part : part + 1, :] = gain[:, span]
    token = rows_f32[...]
    spread = jnp.sum(token * token, keepdims=True) * (1.0 / (16 * TILE))
    normed[me] = (token * lax.rsqrt(spread + 1e-05) * gain_f32[...]).astype(jnp.bfloat16)
    pl.semaphore_wait(barrier, WIDE - 1)

    def gather_line(step):
        return remote(
            normed.at[me],
            normed.at[me],
            norm_line_sent.at[step - 1],
            norm_landed.at[me],
            other_line(step),
        )

    def gather_pair(step):
        place = other_line(step)
        return remote(
            normed.at[place],
            normed.at[place],
            norm_pair_sent.at[step],
            norm_landed.at[place],
            other_row,
        )

    def gather_core(step, a_row):
        place = at(lax.rem(line + step, LINE), a_row, core)
        return remote(
            normed.at[place],
            normed.at[place],
            norm_core_sent.at[step * PAIR + a_row],
            norm_landed.at[place],
            other_core,
        )

    def landed(place):
        remote(
            normed.at[place],
            normed.at[place],
            norm_pair_sent.at[0],
            norm_landed.at[place],
            other_row,
        ).wait_recv()

    def spread_rows(place):
        block = normed[place].astype(jnp.float32)
        for part in range(TILE // LANES):
            tokens[part, pl.ds(place, 16, stride=16), :] = block[:, part * LANES : (part + 1) * LANES]

    for step in (2, 1, 3):
        gather_line(step).start()
    gather_pair(0).start()
    gather_core(0, row).start()
    spread_rows(me)
    for step in (1, 3, 2):
        landed(other_line(step))
        gather_pair(step).start()
        gather_core(step, row).start()
        spread_rows(other_line(step))
    for step in (0, 1, 3, 2):
        place = at(lax.rem(line + step, LINE), 1 - row, core)
        landed(place)
        gather_core(step, 1 - row).start()
        spread_rows(place)
    for step in range(LINE):
        for a_row in range(PAIR):
            place = at(lax.rem(line + step, LINE), a_row, 1 - core)
            landed(place)
            spread_rows(place)

    total[...] = jnp.zeros_like(total)
    message[...] = jnp.zeros_like(message)
    kv_copy.wait()

    def project(index, carry):
        rows = pl.ds(pl.multiple_of(index * 16, 16), 16)
        tile = jnp.concatenate([tokens[part, rows, :] for part in range(TILE // LANES)], axis=1)
        tile = tile.astype(jnp.bfloat16)
        total[:, TILE:] += jnp.dot(
            tile,
            kv_held[pl.ds(pl.multiple_of(index * TILE, TILE), TILE), :],
            preferred_element_type=jnp.float32,
        )
        query_block(index).wait()
        total[:, :TILE] += jnp.dot(tile, ring[index], preferred_element_type=jnp.float32)

        @pl.when(index < 32 - SLOTS)
        def _():
            out_block(index + SLOTS - 16).start()

        return carry

    lax.fori_loop(0, 16, project, 0)
    for part in range(9):
        message[pl.ds(part, 16, stride=16), :] = total[:, part * LANES : (part + 1) * LANES]
    message_out[...] = message[...].astype(jnp.bfloat16).reshape(WIDE, 16, LANES)

    def query_copy(step):
        peer = lax.rem(me + step, WIDE)
        return remote(
            message_out.at[peer],
            message_in.at[me],
            query_sent.at[step],
            query_landed.at[me],
            peer,
        )

    for step in range(1, WIDE):
        query_copy(step).start()
    message_in[me] = message_out[me]

    index = lax.broadcasted_iota(jnp.int32, (1, HD), 1)
    lower = index < HD // 2
    exponent = jnp.where(lower, index, index - HD // 2).astype(jnp.float32)
    inverse = jnp.exp(exponent * (-2.0 * math.log(500000.0) / HD))
    angle = positions[0].astype(jnp.float32) * inverse
    cosine = jnp.cos(angle)
    sine = jnp.sin(angle)
    sine = jnp.where(lower, -sine, sine)
    visible = lax.broadcasted_iota(jnp.int32, scores.shape, 1) < lengths[0]
    factor = 1.0 / math.sqrt(HD)
    keys_copy.wait()
    values_copy.wait()
    for step in range(1, WIDE):
        place = lax.rem(me + step, WIDE)
        remote(
            message_out.at[place],
            message_in.at[place],
            query_sent.at[step],
            query_landed.at[place],
            place,
        ).wait_recv()
    arrived = [message_in[place].astype(jnp.float32) for place in range(WIDE)]
    query = turn(jnp.concatenate([block[:8] for block in arrived], axis=0), cosine, sine)
    query = query.astype(jnp.bfloat16)
    new_keys = jnp.concatenate([block[8:9] for block in arrived[:KVH]], axis=0)
    new_keys = turn(new_keys, cosine, sine).astype(jnp.bfloat16).astype(jnp.float32)
    new_values = jnp.concatenate([block[8:9] for block in arrived[KVH:]], axis=0)

    def per_query(rows):
        return jnp.concatenate(
            [jnp.broadcast_to(rows[head : head + 1], (GROUP, HD)) for head in range(KVH)], axis=0
        )

    for head in range(KVH):
        rows = slice(head * GROUP, (head + 1) * GROUP)
        scores[rows, :] = lax.dot_general(
            query[rows],
            keys_held[:, head * HD : (head + 1) * HD],
            (((1,), (1,)), ((), ())),
            preferred_element_type=jnp.float32,
        )
    fresh = factor * jnp.sum(
        query.astype(jnp.float32) * per_query(new_keys), axis=1, keepdims=True
    )
    scored = jnp.where(visible, factor * scores[...], -1e30)
    highest = jnp.maximum(jnp.max(scored, axis=1, keepdims=True), fresh)
    raised = jnp.exp(scored - highest)
    fresh = jnp.exp(fresh - highest)
    whole = 1.0 / (jnp.sum(raised, axis=1, keepdims=True) + fresh)
    weights = (raised * whole).astype(jnp.bfloat16)
    fresh = (fresh * whole).astype(jnp.bfloat16).astype(jnp.float32)
    attended = jnp.concatenate(
        [
            jnp.dot(
                weights[head * GROUP : (head + 1) * GROUP],
                values_held[:, head * HD : (head + 1) * HD],
                preferred_element_type=jnp.float32,
            )
            for head in range(KVH)
        ],
        axis=0,
    )
    attended = attended + fresh * per_query(new_values)
    heads_out[...] = attended.astype(jnp.bfloat16).astype(jnp.float32)

    def heads_copy(step):
        peer = lax.rem(me + step, WIDE)
        return remote(
            heads_out.at[pl.ds(pl.multiple_of(peer * 8, 8), 8), :],
            heads_in.at[pl.ds(pl.multiple_of(by_core(me) * 8, 8), 8), :],
            heads_sent.at[step],
            heads_landed.at[me],
            peer,
        )

    for step in range(1, WIDE):
        heads_copy(step).start()
    heads_in[pl.ds(pl.multiple_of(by_core(me) * 8, 8), 8), :] = heads_out[
        pl.ds(pl.multiple_of(me * 8, 8), 8), :
    ]
    for step in range(1, WIDE):
        place = lax.rem(me + step, WIDE)
        remote(
            heads_out.at[pl.ds(pl.multiple_of(place * 8, 8), 8), :],
            heads_in.at[pl.ds(pl.multiple_of(by_core(place) * 8, 8), 8), :],
            heads_sent.at[step],
            heads_landed.at[place],
            place,
        ).wait_recv()
    mixed[...] = jnp.concatenate(
        [heads_in[pl.ds(part, 16, stride=8), :] for part in range(8)], axis=1
    ).astype(jnp.bfloat16)

    half = 8 * 16
    quarter = 4 * 16

    def core_copy(chunk):
        away = pl.ds(pl.multiple_of((1 - core) * half, half), half)
        return remote(
            partial.at[chunk, away, :],
            from_core.at[chunk],
            core_sent.at[chunk],
            core_landed.at[chunk],
            other_core,
        )

    def pair_copy(chunk):
        return remote(
            pair_out.at[chunk],
            pair_in.at[chunk],
            pair_sent.at[chunk],
            pair_landed.at[chunk],
            other_row,
        )

    def line_copy(chunk, step):
        goal = lax.rem(line + step, LINE)
        return remote(
            line_out.at[chunk, goal],
            line_in.at[chunk, step - 1],
            line_sent.at[chunk, step - 1],
            line_landed.at[chunk, step - 1],
            other_line(step),
        )

    def multiply(chunk):
        for side in range(2):
            number = chunk * 2 + side
            out_block(number).wait()
            slot = lax.rem(number + 16, SLOTS)
            product = jnp.dot(mixed[...], ring[slot], preferred_element_type=jnp.float32)
            for part in range(TILE // LANES):
                partial[chunk, pl.ds(side * 8 + part, 16, stride=16), :] = product[
                    :, part * LANES : (part + 1) * LANES
                ]
        core_copy(chunk).start()

    def over_cores(chunk):
        core_copy(chunk).wait_recv()
        away, home = (1 - row) * quarter, row * quarter
        base = core * half
        pair_out[chunk] = (
            partial[chunk, pl.ds(pl.multiple_of(base + away, quarter), quarter), :]
            + from_core[chunk, pl.ds(pl.multiple_of(away, quarter), quarter), :]
        ).astype(jnp.bfloat16)
        pair_copy(chunk).start()
        keep[chunk] = (
            partial[chunk, pl.ds(pl.multiple_of(base + home, quarter), quarter), :]
            + from_core[chunk, pl.ds(pl.multiple_of(home, quarter), quarter), :]
        )

    def over_pair(chunk):
        pair_copy(chunk).wait_recv()
        added = keep[chunk] + pair_in[chunk].astype(jnp.float32)
        keep[chunk] = added
        line_out[chunk] = added.astype(jnp.bfloat16).reshape(LINE, 16, LANES)
        for step in (2, 1, 3):
            line_copy(chunk, step).start()

    def over_line(chunk):
        for step in range(1, LINE):
            line_copy(chunk, step).wait_recv()
        added = keep[chunk, pl.ds(pl.multiple_of(line * 16, 16), 16), :]
        for step in range(1, LINE):
            added = added + line_in[chunk, step - 1].astype(jnp.float32)
        out[pl.ds(pl.multiple_of(chunk * 16, 16), 16), :] = added

    def stage(time, carry):
        pl.when(time < STEPS)(lambda: multiply(time))
        for lag, task in ((LAGS[0], over_cores), (LAGS[1], over_pair), (LAGS[2], over_line)):
            pl.when((time >= lag) & (time < STEPS + lag))(lambda lag=lag, task=task: task(time - lag))
        return carry

    lax.fori_loop(0, STEPS + LAGS[2], stage, 0)

    for step in range(1, LINE):
        gather_line(step).wait_send()
    for step in range(LINE):
        gather_pair(step).wait_send()
        for a_row in range(PAIR):
            gather_core(step, a_row).wait_send()
    for step in range(1, WIDE):
        query_copy(step).wait_send()
        heads_copy(step).wait_send()

    def drain(chunk, carry):
        core_copy(chunk).wait_send()
        pair_copy(chunk).wait_send()
        for step in range(1, LINE):
            line_copy(chunk, step).wait_send()
        return carry

    lax.fori_loop(0, STEPS, drain, 0)


def per_device_fused(
    hidden_in,
    norm_gain,
    query_weight,
    kv_weight,
    out_weight,
    cache_keys,
    cache_values,
    lengths,
    positions,
):
    slots = cache_keys.shape[1]
    f32, bf16 = jnp.float32, jnp.bfloat16
    vmem, dma = pltpu.VMEM, pltpu.SemaphoreType.DMA
    summed = pl.pallas_call(
        fused_kernel,
        out_shape=jax.ShapeDtypeStruct((LANES, LANES), f32),
        in_specs=[pl.BlockSpec(memory_space=pltpu.SMEM)] * 2
        + [pl.BlockSpec(memory_space=pltpu.VMEM)] * 2
        + [pl.BlockSpec(memory_space=pl.ANY)] * 5,
        out_specs=pl.BlockSpec(memory_space=pltpu.VMEM),
        scratch_shapes=[
            vmem((SLOTS, TILE, TILE), bf16),
            vmem((16 * TILE, LANES), bf16),
            vmem((slots, KVH * HD), bf16),
            vmem((slots, KVH * HD), bf16),
            vmem((16, TILE), f32),
            vmem((16, TILE), f32),
            vmem((WIDE, 16, TILE), bf16),
            vmem((TILE // LANES, 256, LANES), f32),
            vmem((16, TILE + LANES), f32),
            vmem((WIDE * 16, LANES), f32),
            vmem((WIDE, 16, LANES), bf16),
            vmem((WIDE, 16, LANES), bf16),
            vmem((HQ, slots), f32),
            vmem((WIDE * 8, LANES), f32),
            vmem((WIDE * 8, LANES), f32),
            vmem((16, TILE), bf16),
            vmem((STEPS, 256, LANES), f32),
            vmem((STEPS, 128, LANES), f32),
            vmem((STEPS, 64, LANES), f32),
            vmem((STEPS, 64, LANES), bf16),
            vmem((STEPS, 64, LANES), bf16),
            vmem((STEPS, LINE, 16, LANES), bf16),
            vmem((STEPS, LINE - 1, 16, LANES), bf16),
            dma((SLOTS,)),
            dma,
            dma((2,)),
            dma((LINE - 1,)),
            dma((LINE,)),
            dma((LINE * PAIR,)),
            dma((WIDE,)),
            dma((WIDE,)),
            dma((WIDE,)),
            dma((WIDE,)),
            dma((WIDE,)),
            dma((STEPS,)),
            dma((STEPS,)),
            dma((STEPS,)),
            dma((STEPS,)),
            dma((STEPS, LINE - 1)),
            dma((STEPS, LINE - 1)),
        ],
        compiler_params=pltpu.CompilerParams(
            collective_id=0, has_side_effects=True, vmem_limit_bytes=62 * 1024 * 1024
        ),
        name="decode_attention",
    )(
        lengths,
        positions,
        hidden_in,
        norm_gain.reshape(1, -1),
        query_weight,
        kv_weight,
        out_weight,
        cache_keys,
        cache_values,
    )
    return (hidden_in.astype(f32) + summed.reshape(1, -1)).astype(bf16)


def solution(mesh):
    body = per_device_fused if mesh.shape["wide"] == WIDE else per_device
    return jax.shard_map(
        body,
        mesh=mesh,
        in_specs=(
            P(("groups", "wide"), None),
            P(),
            P(None, "wide"),
            P(None, "wide"),
            P("wide", None),
            P(("groups", "wide"), None, None),
            P(("groups", "wide"), None, None),
            P(("groups", "wide")),
            P(("groups", "wide")),
        ),
        out_specs=P(("groups", "wide"), None),
        check_vma=False,
    )
```

```python
import math

import jax
import jax.numpy as jnp
from jax import lax
from jax.experimental import pallas as pl
from jax.experimental.pallas import tpu as pltpu
from jax.sharding import PartitionSpec as P

HQ = 128
KVH = 8
HD = 128
GROUP = 16


def rms_scale(inputs_wide, norm_gain):
    spread = jnp.mean(inputs_wide * inputs_wide, axis=-1, keepdims=True)
    return inputs_wide * lax.rsqrt(spread + 1e-05) * norm_gain


def rotary(values, places, head_count, head_size):
    grouped = values.reshape(values.shape[0], head_count, head_size)
    halfway = head_size // 2
    indices = jnp.arange(halfway).astype(jnp.float32)
    inverse = jnp.exp(indices * (-2.0 * math.log(500000.0) / head_size))
    angles = places.astype(jnp.float32)[:, None] * inverse[None, :]
    cosine = jnp.cos(angles)[:, None, :]
    sine = jnp.sin(angles)[:, None, :]
    first = grouped[..., :halfway]
    second = grouped[..., halfway:]
    turned = jnp.concatenate(
        [first * cosine - second * sine, second * cosine + first * sine], axis=-1
    )
    return turned.reshape(values.shape)


def attend(query_rows, kv_rows, cache_keys, cache_values, lengths, positions):
    local_rows, slots = (cache_keys.shape[0], cache_keys.shape[1])
    group_size = HQ // KVH
    key_width = KVH * HD
    factor = 1.0 / math.sqrt(HD)
    queries = rotary(query_rows.astype(jnp.float32), positions, HQ, HD).astype(jnp.bfloat16)
    queries = queries.reshape(local_rows, KVH, group_size, HD)
    new_keys = rotary(kv_rows[:, :key_width].astype(jnp.float32), positions, KVH, HD).astype(
        jnp.bfloat16
    )
    new_keys = new_keys.reshape(local_rows, KVH, HD)
    new_values = kv_rows[:, key_width:].reshape(local_rows, KVH, HD)
    old_keys = cache_keys.reshape(local_rows, slots, KVH, HD)
    old_values = cache_values.reshape(local_rows, slots, KVH, HD)
    cached_scores = (
        jnp.einsum("rkgd,rlkd->rkgl", queries, old_keys, preferred_element_type=jnp.float32)
        * factor
    )
    fresh_scores = (
        jnp.einsum("rkgd,rkd->rkg", queries, new_keys, preferred_element_type=jnp.float32) * factor
    )
    visible = jnp.arange(slots)[None, :] < lengths[:, None]
    cached_scores = jnp.where(visible[:, None, None, :], cached_scores, -1e30)
    highest = jnp.maximum(jnp.max(cached_scores, axis=-1), fresh_scores)
    cached_exp = jnp.exp(cached_scores - highest[..., None])
    fresh_exp = jnp.exp(fresh_scores - highest)
    totals = jnp.sum(cached_exp, axis=-1) + fresh_exp
    cached_weights = (cached_exp / totals[..., None]).astype(jnp.bfloat16)
    fresh_weights = (fresh_exp / totals).astype(jnp.bfloat16)
    mixed_values = jnp.einsum(
        "rkgl,rlkd->rkgd", cached_weights, old_values, preferred_element_type=jnp.float32
    )
    mixed_values = (
        mixed_values
        + fresh_weights.astype(jnp.float32)[..., None]
        * new_values.astype(jnp.float32)[:, :, None, :]
    )
    return mixed_values.reshape(local_rows, HQ * HD).astype(jnp.bfloat16)


def per_device(
    hidden_in,
    norm_gain,
    query_weight,
    kv_weight,
    out_weight,
    cache_keys,
    cache_values,
    lengths,
    positions,
):
    inputs_wide = hidden_in.astype(jnp.float32)
    normed = rms_scale(inputs_wide, norm_gain).astype(jnp.bfloat16)
    query_cols = query_weight.shape[1]
    piece = lax.all_gather(normed, "wide", axis=0, tiled=True)
    query_part = jnp.dot(piece, query_weight, preferred_element_type=jnp.float32)
    fresh_part = jnp.dot(piece, kv_weight, preferred_element_type=jnp.float32)
    projected = jnp.concatenate([query_part, fresh_part], axis=1).astype(jnp.bfloat16)
    query_rows, kv_rows = (
        lax.all_to_all(projected[:, :query_cols], "wide", split_axis=0, concat_axis=1, tiled=True),
        lax.all_to_all(projected[:, query_cols:], "wide", split_axis=0, concat_axis=1, tiled=True),
    )
    attended = attend(query_rows, kv_rows, cache_keys, cache_values, lengths, positions)
    by_heads = lax.all_to_all(attended, "wide", split_axis=1, concat_axis=0, tiled=True)
    summed = lax.psum_scatter(
        jnp.dot(by_heads, out_weight, preferred_element_type=jnp.float32),
        "wide",
        scatter_dimension=0,
        tiled=True,
    )
    return (inputs_wide + summed).astype(jnp.bfloat16)


LINE, PAIR, CORES = 4, 2, 2
CHIPS = LINE * PAIR
WIDE = CHIPS * CORES
TILE = 1024
SLOTS = 24
LANES = 128
STEPS = 8
LAGS = (2, 6)


def remote(source, target, sent, landed, peer):
    return pltpu.make_async_remote_copy(
        src_ref=source,
        dst_ref=target,
        send_sem=sent,
        recv_sem=landed,
        device_id={"wide": peer},
        device_id_type=pl.DeviceIdType.MESH,
    )


def turn(values, cosine, sine):
    return values * cosine + pltpu.roll(values, HD // 2, 1) * sine


def fused_kernel(
    lengths,
    positions,
    hidden,
    gain,
    wq,
    wkv,
    wo,
    keys,
    values,
    out,
    ring,
    kv_held,
    keys_held,
    values_held,
    rows_f32,
    gain_f32,
    normed,
    tokens,
    total,
    message,
    message_out,
    message_in,
    scores,
    heads_out,
    heads_in,
    mixed,
    partial,
    from_core,
    chip_out,
    chip_in,
    ring_sem,
    kv_sem,
    cache_sem,
    norm_line_sent,
    norm_pair_sent,
    norm_core_sent,
    norm_landed,
    query_sent,
    query_landed,
    heads_sent,
    heads_landed,
    core_sent,
    core_landed,
    chip_sent,
    chip_landed,
):
    me = lax.axis_index("wide")
    core = lax.rem(me, CORES)
    row = lax.rem(me // CORES, PAIR)
    line = me // (CORES * PAIR)

    def at(a_line, a_row, a_core):
        return (a_line * PAIR + a_row) * CORES + a_core

    def by_core(place):
        return (
            lax.rem(place, CORES) * (PAIR * LINE)
            + lax.rem(place // CORES, PAIR) * LINE
            + place // (CORES * PAIR)
        )

    other_core = at(line, row, 1 - core)
    other_row = at(line, 1 - row, core)

    chip = row * LINE + line

    def on_chip(step, a_core):
        place = lax.rem(chip + step, CHIPS)
        return at(lax.rem(place, LINE), place // LINE, a_core)

    def other_line(step):
        return at(lax.rem(line + step, LINE), row, core)

    def query_block(index):
        return pltpu.make_async_copy(
            wq.at[pl.ds(index * TILE, TILE), :], ring.at[index], ring_sem.at[index]
        )

    def out_block(index):
        slot = lax.rem(index + 16, SLOTS)
        return pltpu.make_async_copy(
            wo.at[:, pl.ds(pl.multiple_of(index * TILE, TILE), TILE)],
            ring.at[slot],
            ring_sem.at[slot],
        )

    barrier = pltpu.get_barrier_semaphore()
    for step in range(1, WIDE):
        pl.semaphore_signal(
            barrier,
            inc=1,
            device_id={"wide": lax.rem(me + step, WIDE)},
            device_id_type=pl.DeviceIdType.MESH,
        )

    kv_copy = pltpu.make_async_copy(wkv, kv_held, kv_sem)
    kv_copy.start()
    for index in range(16):
        query_block(index).start()
    keys_copy = pltpu.make_async_copy(keys.at[0], keys_held, cache_sem.at[0])
    values_copy = pltpu.make_async_copy(values.at[0], values_held, cache_sem.at[1])
    keys_copy.start()
    values_copy.start()

    for part in range(16):
        span = slice(part * TILE, (part + 1) * TILE)
        rows_f32[part : part + 1, :] = hidden[:, span].astype(jnp.float32)
        gain_f32[part : part + 1, :] = gain[:, span]
    token = rows_f32[...]
    spread = jnp.sum(token * token, keepdims=True) * (1.0 / (16 * TILE))
    normed[me] = (token * lax.rsqrt(spread + 1e-05) * gain_f32[...]).astype(jnp.bfloat16)
    pl.semaphore_wait(barrier, WIDE - 1)

    def gather_line(step):
        return remote(
            normed.at[me],
            normed.at[me],
            norm_line_sent.at[step - 1],
            norm_landed.at[me],
            other_line(step),
        )

    def gather_pair(step):
        place = other_line(step)
        return remote(
            normed.at[place],
            normed.at[place],
            norm_pair_sent.at[step],
            norm_landed.at[place],
            other_row,
        )

    def gather_core(step, a_row):
        place = at(lax.rem(line + step, LINE), a_row, core)
        return remote(
            normed.at[place],
            normed.at[place],
            norm_core_sent.at[step * PAIR + a_row],
            norm_landed.at[place],
            other_core,
        )

    def landed(place):
        remote(
            normed.at[place],
            normed.at[place],
            norm_pair_sent.at[0],
            norm_landed.at[place],
            other_row,
        ).wait_recv()

    def spread_rows(place):
        block = normed[place].astype(jnp.float32)
        for part in range(TILE // LANES):
            tokens[part, pl.ds(place, 16, stride=16), :] = block[:, part * LANES : (part + 1) * LANES]

    for step in (2, 1, 3):
        gather_line(step).start()
    gather_pair(0).start()
    gather_core(0, row).start()
    spread_rows(me)
    for step in (1, 3, 2):
        landed(other_line(step))
        gather_pair(step).start()
        gather_core(step, row).start()
        spread_rows(other_line(step))
    for step in (0, 1, 3, 2):
        place = at(lax.rem(line + step, LINE), 1 - row, core)
        landed(place)
        gather_core(step, 1 - row).start()
        spread_rows(place)
    for step in range(LINE):
        for a_row in range(PAIR):
            place = at(lax.rem(line + step, LINE), a_row, 1 - core)
            landed(place)
            spread_rows(place)

    total[...] = jnp.zeros_like(total)
    message[...] = jnp.zeros_like(message)
    kv_copy.wait()

    def project(index, carry):
        rows = pl.ds(pl.multiple_of(index * 16, 16), 16)
        tile = jnp.concatenate([tokens[part, rows, :] for part in range(TILE // LANES)], axis=1)
        tile = tile.astype(jnp.bfloat16)
        total[:, TILE:] += jnp.dot(
            tile,
            kv_held[pl.ds(pl.multiple_of(index * TILE, TILE), TILE), :],
            preferred_element_type=jnp.float32,
        )
        query_block(index).wait()
        total[:, :TILE] += jnp.dot(tile, ring[index], preferred_element_type=jnp.float32)

        out_block(index).start()
        return carry

    lax.fori_loop(0, 16, project, 0)
    for part in range(9):
        message[pl.ds(part, 16, stride=16), :] = total[:, part * LANES : (part + 1) * LANES]
    message_out[...] = message[...].astype(jnp.bfloat16).reshape(WIDE, 16, LANES)

    def query_copy(step):
        peer = lax.rem(me + step, WIDE)
        return remote(
            message_out.at[peer],
            message_in.at[me],
            query_sent.at[step],
            query_landed.at[me],
            peer,
        )

    for step in range(1, WIDE):
        query_copy(step).start()
    message_in[me] = message_out[me]

    index = lax.broadcasted_iota(jnp.int32, (1, HD), 1)
    lower = index < HD // 2
    exponent = jnp.where(lower, index, index - HD // 2).astype(jnp.float32)
    inverse = jnp.exp(exponent * (-2.0 * math.log(500000.0) / HD))
    angle = positions[0].astype(jnp.float32) * inverse
    cosine = jnp.cos(angle)
    sine = jnp.sin(angle)
    sine = jnp.where(lower, -sine, sine)
    visible = lax.broadcasted_iota(jnp.int32, scores.shape, 1) < lengths[0]
    factor = 1.0 / math.sqrt(HD)
    keys_copy.wait()
    values_copy.wait()
    for step in range(1, WIDE):
        place = lax.rem(me + step, WIDE)
        remote(
            message_out.at[place],
            message_in.at[place],
            query_sent.at[step],
            query_landed.at[place],
            place,
        ).wait_recv()
    arrived = [message_in[place].astype(jnp.float32) for place in range(WIDE)]
    query = turn(jnp.concatenate([block[:8] for block in arrived], axis=0), cosine, sine)
    query = query.astype(jnp.bfloat16)
    new_keys = jnp.concatenate([block[8:9] for block in arrived[:KVH]], axis=0)
    new_keys = turn(new_keys, cosine, sine).astype(jnp.bfloat16).astype(jnp.float32)
    new_values = jnp.concatenate([block[8:9] for block in arrived[KVH:]], axis=0)

    def per_query(rows):
        return jnp.concatenate(
            [jnp.broadcast_to(rows[head : head + 1], (GROUP, HD)) for head in range(KVH)], axis=0
        )

    for head in range(KVH):
        rows = slice(head * GROUP, (head + 1) * GROUP)
        scores[rows, :] = lax.dot_general(
            query[rows],
            keys_held[:, head * HD : (head + 1) * HD],
            (((1,), (1,)), ((), ())),
            preferred_element_type=jnp.float32,
        )
    fresh = factor * jnp.sum(
        query.astype(jnp.float32) * per_query(new_keys), axis=1, keepdims=True
    )
    scored = jnp.where(visible, factor * scores[...], -1e30)
    highest = jnp.maximum(jnp.max(scored, axis=1, keepdims=True), fresh)
    raised = jnp.exp(scored - highest)
    fresh = jnp.exp(fresh - highest)
    whole = 1.0 / (jnp.sum(raised, axis=1, keepdims=True) + fresh)
    weights = (raised * whole).astype(jnp.bfloat16)
    fresh = (fresh * whole).astype(jnp.bfloat16).astype(jnp.float32)
    attended = jnp.concatenate(
        [
            jnp.dot(
                weights[head * GROUP : (head + 1) * GROUP],
                values_held[:, head * HD : (head + 1) * HD],
                preferred_element_type=jnp.float32,
            )
            for head in range(KVH)
        ],
        axis=0,
    )
    attended = attended + fresh * per_query(new_values)
    heads_out[...] = attended.astype(jnp.bfloat16).astype(jnp.float32)

    def heads_copy(step):
        peer = lax.rem(me + step, WIDE)
        return remote(
            heads_out.at[pl.ds(pl.multiple_of(peer * 8, 8), 8), :],
            heads_in.at[pl.ds(pl.multiple_of(by_core(me) * 8, 8), 8), :],
            heads_sent.at[step],
            heads_landed.at[me],
            peer,
        )

    for step in range(1, WIDE):
        heads_copy(step).start()
    heads_in[pl.ds(pl.multiple_of(by_core(me) * 8, 8), 8), :] = heads_out[
        pl.ds(pl.multiple_of(me * 8, 8), 8), :
    ]
    for step in range(1, WIDE):
        place = lax.rem(me + step, WIDE)
        remote(
            heads_out.at[pl.ds(pl.multiple_of(place * 8, 8), 8), :],
            heads_in.at[pl.ds(pl.multiple_of(by_core(place) * 8, 8), 8), :],
            heads_sent.at[step],
            heads_landed.at[place],
            place,
        ).wait_recv()
    mixed[...] = jnp.concatenate(
        [heads_in[pl.ds(part, 16, stride=8), :] for part in range(8)], axis=1
    ).astype(jnp.bfloat16)

    half = CHIPS * 16

    def core_copy(chunk):
        away = pl.ds(pl.multiple_of((1 - core) * half, half), half)
        return remote(
            partial.at[chunk, away, :],
            from_core.at[chunk],
            core_sent.at[chunk],
            core_landed.at[chunk],
            other_core,
        )

    def chip_copy(chunk, step):
        return remote(
            chip_out.at[chunk, lax.rem(chip + step, CHIPS)],
            chip_in.at[chunk, step - 1],
            chip_sent.at[chunk, step - 1],
            chip_landed.at[chunk, step - 1],
            on_chip(step, core),
        )

    def multiply(chunk):
        for side in range(2):
            number = chunk * 2 + side
            out_block(number).wait()
            slot = lax.rem(number + 16, SLOTS)
            product = jnp.dot(mixed[...], ring[slot], preferred_element_type=jnp.float32)
            for part in range(TILE // LANES):
                partial[chunk, pl.ds(side * 8 + part, 16, stride=16), :] = product[
                    :, part * LANES : (part + 1) * LANES
                ]
        core_copy(chunk).start()

    def over_cores(chunk):
        core_copy(chunk).wait_recv()
        home = pl.multiple_of(core * half, half)
        added = partial[chunk, pl.ds(home, half), :] + from_core[chunk]
        chip_out[chunk] = added.astype(jnp.bfloat16).reshape(CHIPS, 16, LANES)
        for step in range(1, CHIPS):
            chip_copy(chunk, step).start()

    def over_chips(chunk):
        for step in range(1, CHIPS):
            chip_copy(chunk, step).wait_recv()
        own = pl.multiple_of(chip * 16, 16)
        added = (
            partial[chunk, pl.ds(pl.multiple_of(core * half + own, 16), 16), :]
            + from_core[chunk, pl.ds(own, 16), :]
        )
        for step in range(1, CHIPS):
            added = added + chip_in[chunk, step - 1].astype(jnp.float32)
        out[pl.ds(pl.multiple_of(chunk * 16, 16), 16), :] = added

    def stage(time, carry):
        pl.when(time < STEPS)(lambda: multiply(time))
        for lag, task in ((LAGS[0], over_cores), (LAGS[1], over_chips)):
            pl.when((time >= lag) & (time < STEPS + lag))(lambda lag=lag, task=task: task(time - lag))
        return carry

    lax.fori_loop(0, STEPS + LAGS[1], stage, 0)

    for step in range(1, LINE):
        gather_line(step).wait_send()
    for step in range(LINE):
        gather_pair(step).wait_send()
        for a_row in range(PAIR):
            gather_core(step, a_row).wait_send()
    for step in range(1, WIDE):
        query_copy(step).wait_send()
        heads_copy(step).wait_send()

    def drain(chunk, carry):
        core_copy(chunk).wait_send()
        for step in range(1, CHIPS):
            chip_copy(chunk, step).wait_send()
        return carry

    lax.fori_loop(0, STEPS, drain, 0)


def per_device_fused(
    hidden_in,
    norm_gain,
    query_weight,
    kv_weight,
    out_weight,
    cache_keys,
    cache_values,
    lengths,
    positions,
):
    slots = cache_keys.shape[1]
    f32, bf16 = jnp.float32, jnp.bfloat16
    vmem, dma = pltpu.VMEM, pltpu.SemaphoreType.DMA
    summed = pl.pallas_call(
        fused_kernel,
        out_shape=jax.ShapeDtypeStruct((LANES, LANES), f32),
        in_specs=[pl.BlockSpec(memory_space=pltpu.SMEM)] * 2
        + [pl.BlockSpec(memory_space=pltpu.VMEM)] * 2
        + [pl.BlockSpec(memory_space=pl.ANY)] * 5,
        out_specs=pl.BlockSpec(memory_space=pltpu.VMEM),
        scratch_shapes=[
            vmem((SLOTS, TILE, TILE), bf16),
            vmem((16 * TILE, LANES), bf16),
            vmem((slots, KVH * HD), bf16),
            vmem((slots, KVH * HD), bf16),
            vmem((16, TILE), f32),
            vmem((16, TILE), f32),
            vmem((WIDE, 16, TILE), bf16),
            vmem((TILE // LANES, 256, LANES), f32),
            vmem((16, TILE + LANES), f32),
            vmem((WIDE * 16, LANES), f32),
            vmem((WIDE, 16, LANES), bf16),
            vmem((WIDE, 16, LANES), bf16),
            vmem((HQ, slots), f32),
            vmem((WIDE * 8, LANES), f32),
            vmem((WIDE * 8, LANES), f32),
            vmem((16, TILE), bf16),
            vmem((STEPS, 256, LANES), f32),
            vmem((STEPS, 128, LANES), f32),
            vmem((STEPS, CHIPS, 16, LANES), bf16),
            vmem((STEPS, CHIPS - 1, 16, LANES), bf16),
            dma((SLOTS,)),
            dma,
            dma((2,)),
            dma((LINE - 1,)),
            dma((LINE,)),
            dma((LINE * PAIR,)),
            dma((WIDE,)),
            dma((WIDE,)),
            dma((WIDE,)),
            dma((WIDE,)),
            dma((WIDE,)),
            dma((STEPS,)),
            dma((STEPS,)),
            dma((STEPS, CHIPS - 1)),
            dma((STEPS, CHIPS - 1)),
        ],
        compiler_params=pltpu.CompilerParams(
            collective_id=0, has_side_effects=True, vmem_limit_bytes=62 * 1024 * 1024
        ),
        name="decode_attention",
    )(
        lengths,
        positions,
        hidden_in,
        norm_gain.reshape(1, -1),
        query_weight,
        kv_weight,
        out_weight,
        cache_keys,
        cache_values,
    )
    return (hidden_in.astype(f32) + summed.reshape(1, -1)).astype(bf16)


def solution(mesh):
    body = per_device_fused if mesh.shape["wide"] == WIDE else per_device
    return jax.shard_map(
        body,
        mesh=mesh,
        in_specs=(
            P(("groups", "wide"), None),
            P(),
            P(None, "wide"),
            P(None, "wide"),
            P("wide", None),
            P(("groups", "wide"), None, None),
            P(("groups", "wide"), None, None),
            P(("groups", "wide")),
            P(("groups", "wide")),
        ),
        out_specs=P(("groups", "wide"), None),
        check_vma=False,
    )
```
